512 devices in a mesh: blk: 8 (over x_lo, y), tm: 16 (over z), fsdp: 4 (over x_hi, core).
Axes of the slice: x: 4 (x_hi: 2, x_lo: 2; x = x_hi * 2 + x_lo), y: 4, z: 16, core: 2. Of those that a mesh axis runs over, the one named last changes fastest.
Arguments:
- features: bfloat16 [4, 16, 1280, 512], P('fsdp', 'tm', 'blk'), may hold values from -6 to 6
- neighbours: int32 [1280, 8], P('blk'), may hold values from 0 to 1279, as said below
- conv_taps: float32 [9, 512], replicated, may hold values from -3 to 3
- norm_gain: float32 [512], replicated, may hold values from 0.25 to 1.75
- qkv_weight: bfloat16 [512, 1536], P('fsdp'), as said below
- out_weight: bfloat16 [512, 512], P('fsdp'), may hold values from -0.25 to 0.25
- cotangent: bfloat16 [4, 16, 1280, 512], P('fsdp', 'tm', 'blk'), may hold values from -0.020874023 to 0.020874023
Outputs:
- weight_grads: float32 [1048576], P(('blk', 'tm', 'fsdp'))
The draws below stay inside these ranges and needn't reach their ends.
Inputs may be any that keep to these rules, and one draw needn't show every extreme that they name: `neighbours`: row p holds p - 1, p + 1, three neighbouring pixels near p - 128 and three near p + 128, clipped to the window; every entry lies within 130 of p, and one lies exactly 130 away. `qkv_weight`: projection weights of order 512 ** -0.5 per entry.
All inputs are finite; a program needn't handle non-finite values.
Results may differ from the reference program's by a relative error of at most 0.0086.
Values may be sent and summed in bfloat16 or wider, within the bound.
A program may use at most 64 MiB of HBM per device.

```python
import jax
import jax.numpy as jnp
from jax import lax

C = 512
HEADS = 8
CYCLE = 128
PIX = 1280
FRAMES = 16
SAMPLES = 4
ROWS = 81920


def draw_neighbours(key, part):
    jitter = jax.random.randint(key, (PIX, 2), -1, 2).astype(jnp.int32)
    jitter = jitter.at[0, 1].set(1)
    pixel_ids = jnp.arange(PIX, dtype=jnp.int32)[:, None]
    offsets = jnp.array([-1, 1, -CYCLE - 1, -CYCLE, -CYCLE + 1, CYCLE - 1, CYCLE, CYCLE + 1], dtype=jnp.int32)[None, :]
    extra = jnp.concatenate([jnp.zeros((PIX, 2), jnp.int32), jnp.repeat(jitter[:, 0:1], 3, axis=1), jnp.repeat(jitter[:, 1:2], 3, axis=1)], axis=1)
    return jnp.clip(pixel_ids + offsets + extra, 0, PIX - 1).astype(jnp.int32)


def draw_qkv_weight(key, part):
    base = jax.random.normal(key, (C, 3 * C), jnp.float32) * C ** (-0.5)
    return base.astype(jnp.bfloat16)


def levels(own_key, dims, shards, smallest, top_value):
    factor_of = 1.0
    for dim, shards_of in shards:
        draws = jax.random.uniform(jax.random.fold_in(jax.random.fold_in(own_key, 6), dim), (shards_of,), jnp.float32, smallest / len(shards), top_value / len(shards))
        factor_of = factor_of * jnp.repeat(jnp.exp(draws), dims[dim] // shards_of).reshape((-1,) + (1,) * (len(dims) - 1 - dim))
    return factor_of


def normal_values(stream_key, extent, scale, most, cuts=(), held_as=jnp.bfloat16):
    factor_of = levels(stream_key, extent, cuts, -0.22, 0.18) if cuts else 1.0
    values = jax.random.normal(stream_key, extent, jnp.float32) * scale * factor_of
    return jnp.minimum(jnp.maximum(values, -most), most).astype(held_as)


def setup_inputs(seed: int = 0) -> dict:
    key_of = jax.random.split(jax.random.key(seed), 8)
    features = normal_values(key_of[0], (SAMPLES, FRAMES, PIX, C), 1.0, 6.0, ((0, 4), (1, 16), (2, 8)))
    neighbours = draw_neighbours(jax.random.fold_in(key_of[7], 71), 0)
    conv_taps = normal_values(key_of[2], (9, C), 0.35, 3.0, (), jnp.float32)
    norm_gain = jnp.clip(1.0 + 0.15 * jax.random.normal(key_of[3], (C,), jnp.float32), 0.25, 1.75)
    qkv_weight = draw_qkv_weight(jax.random.fold_in(key_of[7], 71), 0)
    out_weight = normal_values(key_of[5], (C, C), C ** -0.5, 0.25, ((0, 4),))
    cotangent = normal_values(key_of[6], (SAMPLES, FRAMES, PIX, C), (1.0 / ROWS ** 0.5), 0.020874023, ((0, 4), (1, 16), (2, 8)))
    return dict(features=features, neighbours=neighbours, conv_taps=conv_taps, norm_gain=norm_gain, qkv_weight=qkv_weight, out_weight=out_weight, cotangent=cotangent)


def rounded(values):
    return lax.optimization_barrier(values.astype(jnp.bfloat16)).astype(jnp.float32)

def attend_rows(qkv_rows, grad_rows):
    frames, pixels, width = qkv_rows.shape
    channels = width // 3

    def split_heads(block):
        return block.reshape(frames, pixels, HEADS, channels // HEADS).astype(jnp.float32)
    queries = split_heads(qkv_rows[:, :, :channels])
    keys_all = split_heads(qkv_rows[:, :, channels:2 * channels])
    values = split_heads(qkv_rows[:, :, 2 * channels:])
    grads = split_heads(grad_rows)
    scores = jnp.einsum('tpeh,upeh->petu', queries, keys_all) * 0.125
    causal = jnp.arange(frames)[:, None] >= jnp.arange(frames)[None, :]
    masked = jnp.where(causal, scores, -1e+30)
    largest = lax.optimization_barrier(jnp.max(masked, axis=-1, keepdims=True))
    totals = lax.optimization_barrier(jnp.sum(jnp.exp(masked - largest), axis=-1, keepdims=True))
    log_total = largest + jnp.log(totals)
    weights = rounded(jnp.exp(masked - log_total))
    attended = jnp.einsum('petu,upeh->tpeh', weights, values)
    dprob = jnp.einsum('tpeh,upeh->petu', grads, values)
    delta = lax.optimization_barrier(jnp.sum(weights * dprob, axis=-1, keepdims=True))
    dscore = rounded(weights * (dprob - delta) * 0.125)
    grad_query = jnp.einsum('petu,upeh->tpeh', dscore, keys_all)
    grad_key = jnp.einsum('petu,tpeh->upeh', dscore, queries)
    grad_value = jnp.einsum('petu,tpeh->upeh', weights, grads)
    joined = jnp.concatenate([part.reshape(frames, pixels, channels) for part in (grad_query, grad_key, grad_value)], axis=-1)
    return (attended.reshape(frames, pixels, channels).astype(jnp.bfloat16), joined.astype(jnp.bfloat16))

def sample_pass(pair):
    return attend_rows(pair[0], pair[1])

def reference(features, neighbours, conv_taps, norm_gain, qkv_weight, out_weight, cotangent):
    channels = features.shape[-1]
    inputs = features.astype(jnp.float32)
    spatial = conv_taps[0] * inputs
    for column in range(8):
        spatial = spatial + conv_taps[column + 1] * jnp.take(inputs, neighbours[:, column], axis=2)
    hidden_f = rounded(inputs + spatial)
    inverse = lax.rsqrt(lax.optimization_barrier(jnp.mean(hidden_f * hidden_f, axis=-1, keepdims=True)) + 1e-05)
    normed = (hidden_f * inverse * norm_gain).astype(jnp.bfloat16)
    flat_normed = normed.reshape(-1, channels)
    projected = jnp.dot(flat_normed, qkv_weight, preferred_element_type=jnp.float32).astype(jnp.bfloat16)
    projected = projected.reshape(features.shape[:3] + (3 * channels,))
    flat_cot = cotangent.reshape(-1, channels)
    att_grads = jnp.dot(flat_cot, out_weight.T, preferred_element_type=jnp.float32).astype(jnp.bfloat16)
    att_grads = att_grads.reshape(features.shape)
    attended, dqkv = lax.map(sample_pass, (projected, att_grads))
    grad_in = jnp.dot(flat_normed.T, dqkv.reshape(-1, 3 * channels), preferred_element_type=jnp.float32)
    grad_out = jnp.dot(attended.reshape(-1, channels).T, flat_cot, preferred_element_type=jnp.float32)
    return jnp.concatenate([grad_in.reshape(-1), grad_out.reshape(-1)])
```

```python
import functools

import jax
import jax.numpy as jnp
from jax import lax
from jax.experimental import pallas as pl
from jax.experimental.pallas import tpu as pltpu
from jax.sharding import PartitionSpec as P

HEADS = 8
HALO = 130
MESH = pl.DeviceIdType.MESH
F32 = jnp.float32
BF16 = jnp.bfloat16


def reduce_kernel(
    part,
    out,
    core_out,
    core_in,
    xs_out,
    xs_in,
    ys_out,
    ys_in,
    xs_sum,
    ys_sum,
    xs_out2,
    xs_in2,
    ys_out2,
    ys_in2,
    z_sum,
    z_out,
    z_in,
    core_sems,
    one_sems,
    two_sems,
    z_sems,
):
    blk = lax.axis_index("blk")
    zed = lax.axis_index("tm")
    fsdp = lax.axis_index("fsdp")
    x_lo, y = blk // 4, blk % 4
    x_hi, core = fsdp // 2, fsdp % 2
    x = x_hi * 2 + x_lo

    def at_x(to):
        return ((to % 2) * 4 + y, zed, (to // 2) * 2 + core)

    def at_y(to):
        return (x_lo * 4 + to, zed, fsdp)

    def at_z(to):
        return (blk, to, fsdp)

    mate = (blk, zed, x_hi * 2 + 1 - core)
    partners = [mate]
    partners += [at_x((x + d) % 4) for d in (1, 2, 3)]
    partners += [at_y((y + d) % 4) for d in (1, 2, 3)]
    partners += [at_z((zed + d) % 16) for d in range(1, 16)]
    barrier = pltpu.get_barrier_semaphore()
    for partner in partners:
        pl.semaphore_signal(barrier, inc=1, device_id=partner, device_id_type=MESH)

    for hi in range(2):
        for lo in range(2):
            for j in range(4):
                core_out[hi * 2 + lo, j] = part[lo, j, :, hi, 1 - core].astype(BF16)
    pl.semaphore_wait(barrier, len(partners))

    def send(src, dst, sems, slot, to):
        copy = pltpu.make_async_remote_copy(
            src_ref=src,
            dst_ref=dst,
            send_sem=sems.at[0, slot],
            recv_sem=sems.at[1, slot],
            device_id=to,
            device_id_type=MESH,
        )
        copy.start()
        return copy

    first = send(core_out, core_in, core_sems, 0, mate)
    first.wait()

    def chip(hi, lo, j):
        return part[lo, j, :, hi, core] + core_in[hi * 2 + lo, j].astype(F32)

    for hi in range(2):
        for lo in range(2):
            for j in range(4):
                total = chip(hi, lo, j)
                xs_out[hi * 2 + lo, j] = total[:8].astype(BF16)
                ys_out[j, hi * 2 + lo] = total[8:].astype(BF16)
    ones = []
    for d in (2, 1, 3):
        to = (x + d) % 4
        ones.append(send(xs_out.at[to], xs_in.at[d - 1], one_sems, d - 1, at_x(to)))
        to = (y + d) % 4
        ones.append(send(ys_out.at[to], ys_in.at[d - 1], one_sems, d + 2, at_y(to)))
    for j in range(4):
        xs_sum[j] = part[x_lo, j, 0:8, x_hi, core] + core_in[x, j, 0:8].astype(F32)
        ys_sum[j] = part[j % 2, y, 8:16, j // 2, core] + core_in[j, y, 8:16].astype(F32)
    for copy in ones:
        copy.wait_recv()
    for j in range(4):
        total = xs_sum[j]
        for d in range(3):
            total += xs_in[d, j].astype(F32)
        xs_sum[j] = total
        xs_out2[j] = total.astype(BF16)
        total = ys_sum[j]
        for d in range(3):
            total += ys_in[d, j].astype(F32)
        ys_sum[j] = total
        ys_out2[j] = total.astype(BF16)
    twos = []
    for d in (2, 1, 3):
        to = (y + d) % 4
        twos.append(send(xs_out2.at[to], xs_in2.at[d - 1], two_sems, d - 1, at_y(to)))
        to = (x + d) % 4
        twos.append(send(ys_out2.at[to], ys_in2.at[d - 1], two_sems, d + 2, at_x(to)))
    for copy in twos:
        copy.wait_recv()
    low, high = xs_sum[y], ys_sum[x]
    for d in range(3):
        low += xs_in2[d].astype(F32)
        high += ys_in2[d].astype(F32)
    z_sum[0:8] = low
    z_sum[8:16] = high
    z_out[0:8] = low.astype(BF16)
    z_out[8:16] = high.astype(BF16)
    threes = []
    for d in (8, 7, 9, 6, 10, 5, 11, 4, 12, 3, 13, 2, 14, 1, 15):
        to = (zed + d) % 16
        threes.append(send(z_out.at[to], z_in.at[d - 1], z_sems, d - 1, at_z(to)))
    for copy in threes:
        copy.wait_recv()
    total = z_sum[zed]
    for d in range(15):
        total += z_in[d].astype(F32)
    out[...] = total
    for copy in ones + twos + threes:
        copy.wait_send()


def reduce_scatter(summands):
    part = summands.reshape(2, 4, 16, 2, 2, 16, 128)
    tile = (16, 128)
    return pl.pallas_call(
        reduce_kernel,
        out_shape=jax.ShapeDtypeStruct(tile, F32),
        in_specs=[pl.BlockSpec(memory_space=pltpu.VMEM)],
        out_specs=pl.BlockSpec(memory_space=pltpu.VMEM),
        scratch_shapes=[
            pltpu.VMEM((4, 4, 16) + tile, BF16),
            pltpu.VMEM((4, 4, 16) + tile, BF16),
            pltpu.VMEM((4, 4, 8) + tile, BF16),
            pltpu.VMEM((3, 4, 8) + tile, BF16),
            pltpu.VMEM((4, 4, 8) + tile, BF16),
            pltpu.VMEM((3, 4, 8) + tile, BF16),
            pltpu.VMEM((4, 8) + tile, F32),
            pltpu.VMEM((4, 8) + tile, F32),
            pltpu.VMEM((4, 8) + tile, BF16),
            pltpu.VMEM((3, 8) + tile, BF16),
            pltpu.VMEM((4, 8) + tile, BF16),
            pltpu.VMEM((3, 8) + tile, BF16),
            pltpu.VMEM((16,) + tile, F32),
            pltpu.VMEM((16,) + tile, BF16),
            pltpu.VMEM((15,) + tile, BF16),
            pltpu.SemaphoreType.DMA((2, 1)),
            pltpu.SemaphoreType.DMA((2, 6)),
            pltpu.SemaphoreType.DMA((2, 6)),
            pltpu.SemaphoreType.DMA((2, 15)),
        ],
        compiler_params=pltpu.CompilerParams(
            collective_id=0, has_side_effects=True, vmem_limit_bytes=48 * 1024 * 1024
        ),
    )(part).reshape(-1)


def with_halo(cells, sides, width):
    for axis, dim in sides:
        count = lax.axis_size(axis)
        ends = count - 1
        head = lax.slice_in_dim(cells, 0, width, axis=dim)
        tail = lax.slice_in_dim(cells, cells.shape[dim] - width, cells.shape[dim], axis=dim)
        cells = jnp.concatenate(
            [
                lax.ppermute(tail, axis, [(i, (i + 1) % count) for i in range(ends)]),
                cells,
                lax.ppermute(head, axis, [((i + 1) % count, i) for i in range(ends)]),
            ],
            axis=dim,
        )
    return cells


def rounded(values):
    return lax.optimization_barrier(values.astype(jnp.bfloat16)).astype(jnp.float32)


def attend_all(qkv_rows, grad_rows):
    frames, pixels, width = qkv_rows.shape
    channels = width // 3

    def split_heads(block):
        return block.reshape(frames, pixels, HEADS, channels // HEADS).astype(jnp.float32)

    queries = split_heads(qkv_rows[:, :, :channels])
    keys_all = split_heads(qkv_rows[:, :, channels : 2 * channels])
    values = split_heads(qkv_rows[:, :, 2 * channels :])
    grads = split_heads(grad_rows)
    scores = jnp.einsum("tpeh,upeh->petu", queries, keys_all) * 0.125
    causal = jnp.arange(frames)[:, None] >= jnp.arange(frames)[None, :]
    masked = jnp.where(causal, scores, -1e30)
    largest = jnp.max(masked, axis=-1, keepdims=True)
    totals = jnp.sum(jnp.exp(masked - largest), axis=-1, keepdims=True)
    log_total = largest + jnp.log(totals)
    weights = rounded(jnp.exp(masked - log_total))
    attended = jnp.einsum("petu,upeh->tpeh", weights, values)
    dprob = jnp.einsum("tpeh,upeh->petu", grads, values)
    delta = jnp.sum(weights * dprob, axis=-1, keepdims=True)
    dscore = rounded(weights * (dprob - delta) * 0.125)
    grad_query = jnp.einsum("petu,upeh->tpeh", dscore, keys_all)
    grad_key = jnp.einsum("petu,tpeh->upeh", dscore, queries)
    grad_value = jnp.einsum("petu,tpeh->upeh", weights, grads)
    joined = jnp.concatenate(
        [part.reshape(frames, pixels, channels) for part in (grad_query, grad_key, grad_value)],
        axis=-1,
    )
    return (
        attended.reshape(frames, pixels, channels).astype(jnp.bfloat16),
        joined.astype(jnp.bfloat16),
    )


def per_device(features, neighbours, conv_taps, norm_gain, qkv_weight, out_weight, cotangent):
    inputs = features[0, 0]
    upstream = cotangent[0, 0]
    pixels, channels = inputs.shape
    padded = with_halo(inputs, (("blk", 0),), HALO)
    first_pixel = lax.axis_index("blk") * pixels
    local_rows = neighbours - first_pixel + HALO
    inputs_f = inputs.astype(jnp.float32)
    spatial = conv_taps[0] * inputs_f
    for column in range(8):
        spatial = spatial + conv_taps[column + 1] * jnp.take(
            padded, local_rows[:, column], axis=0
        ).astype(jnp.float32)
    hidden_f = rounded(inputs_f + spatial)
    inverse = lax.rsqrt(jnp.mean(hidden_f * hidden_f, axis=-1, keepdims=True) + 1e-05)
    normed = (hidden_f * inverse * norm_gain).astype(jnp.bfloat16)
    full_qkv, full_out = (
        lax.all_gather(qkv_weight, "fsdp", axis=0, tiled=True),
        lax.all_gather(out_weight, "fsdp", axis=0, tiled=True),
    )
    att_grads = jnp.dot(upstream, full_out.T, preferred_element_type=jnp.float32).astype(
        jnp.bfloat16
    )
    swap_normed, swap_grads, swap_upstream = (
        lax.all_to_all(normed[None], "tm", split_axis=1, concat_axis=0, tiled=True),
        lax.all_to_all(att_grads[None], "tm", split_axis=1, concat_axis=0, tiled=True),
        lax.all_to_all(upstream[None], "tm", split_axis=1, concat_axis=0, tiled=True),
    )
    frames = swap_normed.shape[0]
    few_pixels = swap_normed.shape[1]
    flat_normed = swap_normed.reshape(-1, channels)
    qkv_rows = jnp.dot(flat_normed, full_qkv, preferred_element_type=jnp.float32).astype(
        jnp.bfloat16
    )
    qkv_rows = qkv_rows.reshape(frames, few_pixels, 3 * channels)
    attended_x, dqkv_x = attend_all(qkv_rows, swap_grads)
    grad_in = jnp.einsum(
        "pc,pd->cd",
        flat_normed,
        dqkv_x.reshape(-1, 3 * channels),
        preferred_element_type=jnp.float32,
    )
    grad_out = jnp.einsum(
        "pc,pd->cd",
        attended_x.reshape(-1, channels),
        swap_upstream.reshape(-1, channels),
        preferred_element_type=jnp.float32,
    )
    summands = jnp.concatenate([grad_in.reshape(-1), grad_out.reshape(-1)])
    return reduce_scatter(summands)


def solution(mesh):
    return jax.shard_map(
        per_device,
        mesh=mesh,
        in_specs=(
            P("fsdp", "tm", "blk", None),
            P("blk", None),
            P(),
            P(),
            P("fsdp", None),
            P("fsdp", None),
            P("fsdp", "tm", "blk", None),
        ),
        out_specs=P(("blk", "tm", "fsdp")),
        check_vma=False,
    )
```

```python
import jax
import jax.numpy as jnp
from jax import lax
from jax.experimental import pallas as pl
from jax.experimental.pallas import tpu as pltpu
from jax.sharding import PartitionSpec as P

MESH = pl.DeviceIdType.MESH
F32 = jnp.float32
BF16 = jnp.bfloat16
EDGE = 144
BAND = 160
NEAR = 512
GROUP = 16
GROUPS = BAND // GROUP
ROWS = 16 * GROUP
TILE = (16, 128)


def dot(a, b):
    return lax.dot_general(a, b, (((1,), (0,)), ((), ())), preferred_element_type=F32)


def dot_nt(a, b):
    return lax.dot_general(a, b, (((1,), (1,)), ((), ())), preferred_element_type=F32)


def hidden_rows(near, inputs, local, taps):
    rows = inputs.shape[0]
    inputs = inputs.astype(F32)
    spatial = taps[0:1] * inputs
    column = lax.broadcasted_iota(jnp.int32, (rows, NEAR), 1)
    for k in range(8):
        pick = jnp.where(local[:, k : k + 1] == column, 1.0, 0.0).astype(BF16)
        spatial += taps[k + 1 : k + 2] * dot(pick, near)
    return (inputs + spatial).astype(BF16)


def normalized(hidden, gain):
    hidden = hidden.astype(F32)
    inverse = lax.rsqrt(jnp.mean(hidden * hidden, axis=-1, keepdims=True) + 1e-05)
    return (hidden * inverse * gain).astype(BF16)


def causal_bias():
    row = lax.broadcasted_iota(jnp.int32, (ROWS, ROWS), 0)
    col = lax.broadcasted_iota(jnp.int32, (ROWS, ROWS), 1)
    same = row % GROUP == col % GROUP
    return jnp.where(same & (col <= row), 0.0, -1e30).astype(F32)


def attend_pair(q, k, v, g, bias):
    lane = lax.broadcasted_iota(jnp.int32, q.shape, 1)
    sub = lax.broadcasted_iota(jnp.int32, q.shape[::-1], 0)
    q_t, v_t, g_t = q.T, v.T, g.T
    att_t = dq = dk_t = dv_t = 0.0
    for half in range(2):
        ours = lane // 64 == half
        ours_t = sub // 64 == half
        zero = jnp.zeros((), BF16)
        eighth = jnp.asarray(0.125, BF16)
        scores = dot_nt(jnp.where(ours, q * eighth, zero), k) + bias
        raised = jnp.exp(scores - jnp.max(scores, axis=-1, keepdims=True))
        weights = (raised * (1.0 / jnp.sum(raised, axis=-1, keepdims=True))).astype(BF16)
        dprob = dot_nt(jnp.where(ours, g, zero), v)
        wide = weights.astype(F32)
        delta = jnp.sum(wide * dprob, axis=-1, keepdims=True)
        dscore = (wide * (dprob - delta)).astype(BF16)
        att_t += dot_nt(jnp.where(ours_t, v_t, zero), weights)
        dq += dot(dscore, jnp.where(ours, k * eighth, zero))
        dk_t += dot(jnp.where(ours_t, q_t * eighth, zero), dscore)
        dv_t += dot(jnp.where(ours_t, g_t, zero), weights)
    return att_t.astype(BF16), dq.astype(BF16), dk_t.astype(BF16), dv_t.astype(BF16)


def group_of(zed, core):
    place = (zed + 16 - 2 * core) % 16
    group = (GROUPS * place + 15) // 16
    return jnp.minimum(group, GROUPS - 1), (16 * group) // GROUPS == place


def kernel(
    features,
    neighbours,
    taps,
    gain,
    qkv_shard,
    out_shard,
    cotangent,
    out,
    near,
    normed_out,
    normed_in,
    cot_in,
    qkv_all,
    out_all,
    projected,
    bias,
    att_t,
    dq_all,
    dkv_t,
    part,
    core_out,
    core_in,
    xs_out,
    xs_in,
    ys_out,
    ys_in,
    xs_sum,
    ys_sum,
    xs_out2,
    xs_in2,
    ys_out2,
    ys_in2,
    z_sum,
    z_out,
    z_in,
    halo_sems,
    weight_sems,
    cot_sems,
    normed_sems,
    core_sems,
    one_sems,
    two_sems,
    z_sems,
):
    blk = lax.axis_index("blk")
    zed = lax.axis_index("tm")
    fsdp = lax.axis_index("fsdp")
    x_lo, y = blk // 4, blk % 4
    x_hi, core = fsdp // 2, fsdp % 2
    x = x_hi * 2 + x_lo
    group, active = group_of(zed, core)

    def at_x(to):
        return ((to % 2) * 4 + y, zed, (to // 2) * 2 + core)

    def at_y(to):
        return (x_lo * 4 + to, zed, fsdp)

    def at_z(to):
        return (blk, to, fsdp)

    mate = (blk, zed, x_hi * 2 + 1 - core)
    facing = ((1 - x_lo) * 4 + y, zed, (1 - x_hi) * 2 + core)
    partners = [mate]
    partners += [at_x((x + d) % 4) for d in (1, 2, 3)]
    partners += [at_y((y + d) % 4) for d in (1, 2, 3)]
    partners += [at_z((zed + d) % 16) for d in range(1, 16)]
    barrier = pltpu.get_barrier_semaphore()

    def greet(to):
        pl.semaphore_signal(barrier, inc=1, device_id=to, device_id_type=MESH)

    for partner in partners:
        greet(partner)

    @pl.when(blk == 3)
    def _():
        greet((4, zed, fsdp))

    @pl.when(blk == 4)
    def _():
        greet((3, zed, fsdp))

    def remote(src, dst, sems, slot, to):
        return pltpu.make_async_remote_copy(
            src_ref=src,
            dst_ref=dst,
            send_sem=sems.at[0, slot],
            recv_sem=sems.at[1, slot],
            device_id=to,
            device_id_type=MESH,
        )

    def send(*args):
        copy = remote(*args)
        copy.start()
        return copy

    near[EDGE : EDGE + BAND] = features[...]
    near[2 * EDGE + BAND :] = jnp.zeros((NEAR - 2 * EDGE - BAND, 512), BF16)

    @pl.when(blk == 0)
    def _():
        near[0:EDGE] = jnp.zeros((EDGE, 512), BF16)

    @pl.when(blk == 7)
    def _():
        near[EDGE + BAND : 2 * EDGE + BAND] = jnp.zeros((EDGE, 512), BF16)

    @pl.when(active)
    def _():
        bias[...] = causal_bias()
        cot_in[zed] = cotangent[group]
    shard = pl.ds(pl.multiple_of(fsdp * 128, 128), 128)
    qkv_all[shard] = qkv_shard[...]
    out_all[shard] = out_shard[...]

    extra = jnp.where((blk == 3) | (blk == 4), 1, 0)
    pl.semaphore_wait(barrier, len(partners) + extra)

    up = remote(
        features.at[0:EDGE], near.at[EDGE + BAND : 2 * EDGE + BAND], halo_sems, 0,
        (jnp.maximum(blk - 1, 0), zed, fsdp),
    )
    down = remote(
        features.at[BAND - EDGE : BAND], near.at[0:EDGE], halo_sems, 1,
        (jnp.minimum(blk + 1, 7), zed, fsdp),
    )

    @pl.when(blk > 0)
    def _():
        up.start()

    @pl.when(blk < 7)
    def _():
        down.start()

    far_first = (8, 7, 9, 6, 10, 5, 11, 4, 12, 3, 13, 2, 14, 1, 15)

    def exchange(source, target, sems):
        copies = []
        for d in far_first:
            to = (zed + d) % 16
            theirs, wanted = group_of(to, core)
            copy = remote(source.at[theirs], target.at[zed], sems, d - 1, at_z(to))
            copies.append((copy, wanted))
            pl.when(wanted)(copy.start)
        return copies

    def arrivals(target, sems):
        for d in far_first:
            come = (zed + 16 - d) % 16
            remote(target.at[come], target.at[come], sems, d - 1, at_z(come)).wait_recv()

    cot_copies = exchange(cotangent, cot_in, cot_sems)
    weight_copies = [
        send(qkv_shard, qkv_all.at[shard], weight_sems, 0, facing),
        send(out_shard, out_all.at[shard], weight_sems, 1, facing),
        send(qkv_shard, qkv_all.at[shard], weight_sems, 2, mate),
        send(out_shard, out_all.at[shard], weight_sems, 3, mate),
    ]

    @pl.when(blk > 0)
    def _():
        down.wait_recv()

    @pl.when(blk < 7)
    def _():
        up.wait_recv()

    first_pixel = blk * BAND
    half_rows = BAND // 2
    for part_of in range(2):
        rows = slice(part_of * half_rows, (part_of + 1) * half_rows)
        local = neighbours[rows] - first_pixel + EDGE
        hidden = hidden_rows(near[...], features[rows], local, taps)
        groups = slice(part_of * GROUPS // 2, (part_of + 1) * GROUPS // 2)
        normed_out[groups] = normalized(hidden, gain[...]).reshape(GROUPS // 2, GROUP, 512)
    normed_copies = exchange(normed_out, normed_in, normed_sems)

    @pl.when(active)
    def _():
        normed_in[zed] = normed_out[group]

    facing_shard = pl.ds(pl.multiple_of(((1 - x_hi) * 2 + core) * 128, 128), 128)
    passed = [
        (qkv_all.at[facing_shard], weight_sems, 4, mate),
        (out_all.at[facing_shard], weight_sems, 5, mate),
    ]
    weight_copies[0].wait_recv()
    weight_copies[1].wait_recv()
    weight_copies += [send(ref, ref, sems, slot, to) for ref, sems, slot, to in passed]
    for copy in weight_copies[2:]:
        copy.wait_recv()

    @pl.when(active)
    def _():
        arrivals(cot_in, cot_sems)
        cots = cot_in[...].reshape(ROWS, 512)
        grads = dot_nt(cots, out_all[...]).astype(BF16)
        arrivals(normed_in, normed_sems)
        normed = normed_in[...].reshape(ROWS, 512)
        for j in range(6):
            block = slice(256 * j, 256 * j + 256)
            projected[:, block] = dot(normed, qkv_all[:, block]).astype(BF16)
        for pair in range(4):
            cols = slice(128 * pair, 128 * pair + 128)
            att, dq, dk, dv = attend_pair(
                projected[:, 128 * pair : 128 * pair + 128],
                projected[:, 512 + 128 * pair : 640 + 128 * pair],
                projected[:, 1024 + 128 * pair : 1152 + 128 * pair],
                grads[:, cols],
                bias[...],
            )
            att_t[cols] = att
            dq_all[:, cols] = dq
            dkv_t[128 * pair : 128 * pair + 128] = dk
            dkv_t[512 + 128 * pair : 640 + 128 * pair] = dv
        normed_t = normed.T
        for r in range(4):
            rows = slice(128 * r, 128 * r + 128)
            grad_q = dot(normed_t[rows], dq_all[...])
            grad_kv = dot_nt(normed_t[rows], dkv_t[...])
            for j in range(12):
                block = grad_q if j < 4 else grad_kv
                at = j if j < 4 else j - 4
                part[pl.ds(1536 * r + j, 128, stride=12), :] = block[:, 128 * at : 128 * at + 128]
            grad_o = dot(att_t[rows], cots)
            for j in range(4):
                part[pl.ds(6144 + 512 * r + j, 128, stride=4), :] = grad_o[
                    :, 128 * j : 128 * j + 128
                ]

    @pl.when(jnp.logical_not(active))
    def _():
        part[...] = jnp.zeros_like(part)

    def chunks(lo, j, first, count, hi, c):
        start = (((lo * 4 + j) * 16 + first) * 4 + hi * 2 + c) * 16
        return jnp.stack(
            [part[pl.ds(pl.multiple_of(start + i * 64, 16), 16), :] for i in range(count)]
        )

    for hi in range(2):
        for lo in range(2):
            for j in range(4):
                core_out[hi * 2 + lo, j] = chunks(lo, j, 0, 16, hi, 1 - core).astype(BF16)
    first = send(core_out, core_in, core_sems, 0, mate)
    first.wait()

    for hi in range(2):
        for lo in range(2):
            for j in range(4):
                total = chunks(lo, j, 0, 16, hi, core) + core_in[hi * 2 + lo, j].astype(F32)
                xs_out[hi * 2 + lo, j] = total[:8].astype(BF16)
                ys_out[j, hi * 2 + lo] = total[8:].astype(BF16)
    ones = []
    for d in (2, 1, 3):
        to = (x + d) % 4
        ones.append(send(xs_out.at[to], xs_in.at[d - 1], one_sems, d - 1, at_x(to)))
        to = (y + d) % 4
        ones.append(send(ys_out.at[to], ys_in.at[d - 1], one_sems, d + 2, at_y(to)))
    for j in range(4):
        xs_sum[j] = chunks(x_lo, j, 0, 8, x_hi, core) + core_in[x, j, 0:8].astype(F32)
        ys_sum[j] = chunks(j % 2, y, 8, 8, j // 2, core) + core_in[j, y, 8:16].astype(F32)
    for copy in ones:
        copy.wait_recv()
    for j in range(4):
        total = xs_sum[j]
        for d in range(3):
            total += xs_in[d, j].astype(F32)
        xs_sum[j] = total
        xs_out2[j] = total.astype(BF16)
        total = ys_sum[j]
        for d in range(3):
            total += ys_in[d, j].astype(F32)
        ys_sum[j] = total
        ys_out2[j] = total.astype(BF16)
    twos = []
    for d in (2, 1, 3):
        to = (y + d) % 4
        twos.append(send(xs_out2.at[to], xs_in2.at[d - 1], two_sems, d - 1, at_y(to)))
        to = (x + d) % 4
        twos.append(send(ys_out2.at[to], ys_in2.at[d - 1], two_sems, d + 2, at_x(to)))
    for copy in twos:
        copy.wait_recv()
    low, high = xs_sum[y], ys_sum[x]
    for d in range(3):
        low += xs_in2[d].astype(F32)
        high += ys_in2[d].astype(F32)
    z_sum[0:8] = low
    z_sum[8:16] = high
    z_out[0:8] = low.astype(BF16)
    z_out[8:16] = high.astype(BF16)
    threes = []
    for d in far_first:
        to = (zed + d) % 16
        threes.append(send(z_out.at[to], z_in.at[d - 1], z_sems, d - 1, at_z(to)))
    for copy in threes:
        copy.wait_recv()
    total = z_sum[zed]
    for d in range(15):
        total += z_in[d].astype(F32)
    out[...] = total

    for copy in weight_copies + ones + twos + threes:
        copy.wait_send()
    for copy, wanted in cot_copies + normed_copies:
        pl.when(wanted)(copy.wait_send)

    @pl.when(blk > 0)
    def _():
        up.wait_send()

    @pl.when(blk < 7)
    def _():
        down.wait_send()


def per_device(features, neighbours, conv_taps, norm_gain, qkv_weight, out_weight, cotangent):
    vmem = pl.BlockSpec(memory_space=pltpu.VMEM)

    def pair(count):
        return pltpu.SemaphoreType.DMA((2, count))

    result = pl.pallas_call(
        kernel,
        out_shape=jax.ShapeDtypeStruct(TILE, F32),
        in_specs=[vmem] * 7,
        out_specs=vmem,
        scratch_shapes=[
            pltpu.VMEM((NEAR, 512), BF16),
            pltpu.VMEM((GROUPS, GROUP, 512), BF16),
            pltpu.VMEM((16, GROUP, 512), BF16),
            pltpu.VMEM((16, GROUP, 512), BF16),
            pltpu.VMEM((512, 1536), BF16),
            pltpu.VMEM((512, 512), BF16),
            pltpu.VMEM((ROWS, 1536), BF16),
            pltpu.VMEM((ROWS, ROWS), F32),
            pltpu.VMEM((512, ROWS), BF16),
            pltpu.VMEM((ROWS, 512), BF16),
            pltpu.VMEM((1024, ROWS), BF16),
            pltpu.VMEM((8192, 128), F32),
            pltpu.VMEM((4, 4, 16) + TILE, BF16),
            pltpu.VMEM((4, 4, 16) + TILE, BF16),
            pltpu.VMEM((4, 4, 8) + TILE, BF16),
            pltpu.VMEM((3, 4, 8) + TILE, BF16),
            pltpu.VMEM((4, 4, 8) + TILE, BF16),
            pltpu.VMEM((3, 4, 8) + TILE, BF16),
            pltpu.VMEM((4, 8) + TILE, F32),
            pltpu.VMEM((4, 8) + TILE, F32),
            pltpu.VMEM((4, 8) + TILE, BF16),
            pltpu.VMEM((3, 8) + TILE, BF16),
            pltpu.VMEM((4, 8) + TILE, BF16),
            pltpu.VMEM((3, 8) + TILE, BF16),
            pltpu.VMEM((16,) + TILE, F32),
            pltpu.VMEM((16,) + TILE, BF16),
            pltpu.VMEM((15,) + TILE, BF16),
            pair(2),
            pair(6),
            pair(15),
            pair(15),
            pair(1),
            pair(6),
            pair(6),
            pair(15),
        ],
        compiler_params=pltpu.CompilerParams(
            collective_id=0, has_side_effects=True, vmem_limit_bytes=48 * 1024 * 1024
        ),
    )(
        features.reshape(BAND, 512),
        neighbours,
        conv_taps,
        norm_gain.reshape(1, 512),
        qkv_weight,
        out_weight,
        cotangent.reshape(GROUPS, GROUP, 512),
    )
    return result.reshape(-1)


def solution(mesh):
    return jax.shard_map(
        per_device,
        mesh=mesh,
        in_specs=(
            P("fsdp", "tm", "blk", None),
            P("blk", None),
            P(),
            P(),
            P("fsdp", None),
            P("fsdp", None),
            P("fsdp", "tm", "blk", None),
        ),
        out_specs=P(("blk", "tm", "fsdp")),
        check_vma=False,
    )
```

```python
import jax
import jax.numpy as jnp
from jax import lax
from jax.experimental import pallas as pl
from jax.experimental.pallas import tpu as pltpu
from jax.sharding import PartitionSpec as P

MESH = pl.DeviceIdType.MESH
F32 = jnp.float32
BF16 = jnp.bfloat16
EDGE = 144
BAND = 160
NEAR = 512
GROUP = 16
GROUPS = BAND // GROUP
ROWS = 16 * GROUP
TILE = (16, 128)


def dot(a, b):
    return lax.dot_general(a, b, (((1,), (0,)), ((), ())), preferred_element_type=F32)


def dot_nt(a, b):
    return lax.dot_general(a, b, (((1,), (1,)), ((), ())), preferred_element_type=F32)


def hidden_rows(near, inputs, local, taps):
    rows = inputs.shape[0]
    inputs = inputs.astype(F32)
    spatial = taps[0:1] * inputs
    column = lax.broadcasted_iota(jnp.int32, (rows, NEAR), 1)
    for k in range(8):
        pick = jnp.where(local[:, k : k + 1] == column, 1.0, 0.0).astype(BF16)
        spatial += taps[k + 1 : k + 2] * dot(pick, near)
    return (inputs + spatial).astype(BF16)


def normalized(hidden, gain):
    hidden = hidden.astype(F32)
    inverse = lax.rsqrt(jnp.mean(hidden * hidden, axis=-1, keepdims=True) + 1e-05)
    return (hidden * inverse * gain).astype(BF16)


def causal_bias():
    row = lax.broadcasted_iota(jnp.int32, (ROWS, ROWS), 0)
    col = lax.broadcasted_iota(jnp.int32, (ROWS, ROWS), 1)
    same = row % GROUP == col % GROUP
    return jnp.where(same & (col <= row), 0.0, -1e30).astype(F32)


def attend_pair(q, k, v, g, bias):
    lane = lax.broadcasted_iota(jnp.int32, q.shape, 1)
    sub = lax.broadcasted_iota(jnp.int32, q.shape[::-1], 0)
    q_t, v_t, g_t = q.T, v.T, g.T
    att_t = dq = dk_t = dv_t = 0.0
    for half in range(2):
        ours = lane // 64 == half
        ours_t = sub // 64 == half
        zero = jnp.zeros((), BF16)
        eighth = jnp.asarray(0.125, BF16)
        scores = dot_nt(jnp.where(ours, q * eighth, zero), k) + bias
        raised = jnp.exp(scores - jnp.max(scores, axis=-1, keepdims=True))
        weights = (raised * (1.0 / jnp.sum(raised, axis=-1, keepdims=True))).astype(BF16)
        dprob = dot_nt(jnp.where(ours, g, zero), v)
        wide = weights.astype(F32)
        delta = jnp.sum(wide * dprob, axis=-1, keepdims=True)
        dscore = (wide * (dprob - delta)).astype(BF16)
        att_t += dot_nt(jnp.where(ours_t, v_t, zero), weights)
        dq += dot(dscore, jnp.where(ours, k * eighth, zero))
        dk_t += dot(jnp.where(ours_t, q_t * eighth, zero), dscore)
        dv_t += dot(jnp.where(ours_t, g_t, zero), weights)
    return att_t.astype(BF16), dq.astype(BF16), dk_t.astype(BF16), dv_t.astype(BF16)


def place_of(group):
    return (16 * group) // GROUPS


def group_of(zed):
    group = jnp.minimum((GROUPS * zed + 15) // 16, GROUPS - 1)
    return group, place_of(group) == zed


def kernel(
    features,
    neighbours,
    taps_in,
    gain_in,
    qkv_shard,
    out_shard,
    cotangent,
    out,
    near,
    nearby,
    taps,
    gain,
    normed_out,
    normed_in,
    cot_in,
    qkv_all,
    out_all,
    projected,
    bias,
    att_t,
    dq_all,
    dkv_t,
    part,
    core_out,
    core_in,
    out_1,
    in_1,
    sum_1,
    out_2,
    in_2,
    z_sum,
    z_out,
    z_in,
    local_sems,
    halo_sems,
    weight_sems,
    cot_sems,
    normed_sems,
    core_sems,
    one_sems,
    two_sems,
    z_sems,
):
    blk = lax.axis_index("blk")
    zed = lax.axis_index("tm")
    fsdp = lax.axis_index("fsdp")
    x_lo, y = blk // 4, blk % 4
    x_hi, core = fsdp // 2, fsdp % 2
    x = x_hi * 2 + x_lo
    group, active = group_of(zed)

    def at_x(to):
        return ((to % 2) * 4 + y, zed, (to // 2) * 2 + core)

    def at_y(to):
        return (x_lo * 4 + to, zed, fsdp)

    def at_z(to):
        return (blk, to, fsdp)

    mate = (blk, zed, x_hi * 2 + 1 - core)
    facing = ((1 - x_lo) * 4 + y, zed, (1 - x_hi) * 2 + core)
    partners = [mate]
    partners += [at_x((x + d) % 4) for d in (1, 2, 3)]
    partners += [at_y((y + d) % 4) for d in (1, 2, 3)]
    partners += [at_z((zed + d) % 16) for d in range(1, 16)]
    barrier = pltpu.get_barrier_semaphore()

    def greet(to):
        pl.semaphore_signal(barrier, inc=1, device_id=to, device_id_type=MESH)

    for partner in partners:
        greet(partner)

    @pl.when(blk == 3)
    def _():
        greet((4, zed, fsdp))

    @pl.when(blk == 4)
    def _():
        greet((3, zed, fsdp))

    def remote(src, dst, send_sem, recv_sem, to):
        return pltpu.make_async_remote_copy(
            src_ref=src,
            dst_ref=dst,
            send_sem=send_sem,
            recv_sem=recv_sem,
            device_id=to,
            device_id_type=MESH,
        )

    def send(src, dst, sems, slot, to):
        copy = remote(src, dst, sems.at[0, slot], sems.at[1, slot], to)
        copy.start()
        return copy

    shard = pl.ds(pl.multiple_of(fsdp * 128, 128), 128)
    owned = [
        pltpu.make_async_copy(src, dst, local_sems.at[i])
        for i, (src, dst) in enumerate(
            (
                (features, near.at[EDGE : EDGE + BAND]),
                (neighbours, nearby),
                (taps_in, taps),
                (gain_in, gain),
            )
        )
    ]
    held = [
        pltpu.make_async_copy(src, dst, local_sems.at[4 + i])
        for i, (src, dst) in enumerate(
            (
                (cotangent.at[group], cot_in.at[zed]),
                (qkv_shard, qkv_all.at[shard]),
                (out_shard, out_all.at[shard]),
            )
        )
    ]
    for copy in owned:
        copy.start()

    @pl.when(active)
    def _():
        for copy in held:
            copy.start()

    near[2 * EDGE + BAND :] = jnp.zeros((NEAR - 2 * EDGE - BAND, 512), BF16)
    z_in[...] = jnp.zeros_like(z_in)

    @pl.when(blk == 0)
    def _():
        near[0:EDGE] = jnp.zeros((EDGE, 512), BF16)

    @pl.when(blk == 7)
    def _():
        near[EDGE + BAND : 2 * EDGE + BAND] = jnp.zeros((EDGE, 512), BF16)

    @pl.when(active)
    def _():
        bias[...] = causal_bias()

    @pl.when(jnp.logical_not(active))
    def _():
        z_sum[...] = jnp.zeros_like(z_sum)

    for copy in owned:
        copy.wait()

    extra = jnp.where((blk == 3) | (blk == 4), 1, 0)
    pl.semaphore_wait(barrier, len(partners) + extra)

    up = remote(
        near.at[EDGE : 2 * EDGE],
        near.at[EDGE + BAND : 2 * EDGE + BAND],
        halo_sems.at[0, 0],
        halo_sems.at[1, 0],
        (jnp.maximum(blk - 1, 0), zed, fsdp),
    )
    down = remote(
        near.at[BAND : EDGE + BAND],
        near.at[0:EDGE],
        halo_sems.at[0, 1],
        halo_sems.at[1, 1],
        (jnp.minimum(blk + 1, 7), zed, fsdp),
    )

    @pl.when(blk > 0)
    def _():
        up.start()

    @pl.when(blk < 7)
    def _():
        down.start()

    def exchange(source, target, sems, first, count):
        copies = []
        for k in range(count):
            theirs = first + (k + zed) % count
            to = place_of(theirs)
            copy = remote(
                source.at[theirs], target.at[zed], sems.at[0, theirs], sems.at[1, zed], at_z(to)
            )
            other = to != zed
            copies.append((copy, other))
            pl.when(other)(copy.start)
        return copies

    def arrivals(target, sems):
        for come in range(16):
            copy = remote(
                target.at[come], target.at[come], sems.at[0, 0], sems.at[1, come], at_z(come)
            )
            pl.when(come != zed)(copy.wait_recv)

    weight_copies = [
        remote(src, dst.at[shard], weight_sems.at[0, i], weight_sems.at[1, i], to)
        for i, (src, dst, to) in enumerate(
            (
                (qkv_shard, qkv_all, facing),
                (out_shard, out_all, facing),
                (qkv_shard, qkv_all, mate),
                (out_shard, out_all, mate),
            )
        )
    ]

    @pl.when(active)
    def _():
        for copy in weight_copies:
            copy.start()

    cot_copies = exchange(cotangent, cot_in, cot_sems, 0, GROUPS)
    local_all = nearby[...].T - (blk * BAND - EDGE)

    @pl.when(blk > 0)
    def _():
        down.wait_recv()

    @pl.when(blk < 7)
    def _():
        up.wait_recv()

    normed_copies = []
    half_rows, half_groups = BAND // 2, GROUPS // 2
    for half in range(2):
        rows = slice(half * half_rows, (half + 1) * half_rows)
        own = near[EDGE + half * half_rows : EDGE + (half + 1) * half_rows]
        hidden = hidden_rows(near[...], own, local_all[rows], taps)
        normed_out[half * half_groups : (half + 1) * half_groups] = normalized(
            hidden, gain[...]
        ).reshape(half_groups, GROUP, 512)
        normed_copies += exchange(
            normed_out, normed_in, normed_sems, half * half_groups, half_groups
        )

    @pl.when(active)
    def _():
        normed_in[zed] = normed_out[group]
        facing_shard = pl.ds(pl.multiple_of(((1 - x_hi) * 2 + core) * 128, 128), 128)
        weight_copies[0].wait_recv()
        weight_copies[1].wait_recv()
        passed = [
            send(qkv_all.at[facing_shard], qkv_all.at[facing_shard], weight_sems, 4, mate),
            send(out_all.at[facing_shard], out_all.at[facing_shard], weight_sems, 5, mate),
        ]
        for copy in held:
            copy.wait()
        for copy in weight_copies[2:] + passed:
            copy.wait_recv()
        arrivals(cot_in, cot_sems)
        cots = cot_in[...].reshape(ROWS, 512)
        grads = dot_nt(cots, out_all[...]).astype(BF16)
        arrivals(normed_in, normed_sems)
        normed = normed_in[...].reshape(ROWS, 512)
        for j in range(6):
            block = slice(256 * j, 256 * j + 256)
            projected[:, block] = dot(normed, qkv_all[:, block]).astype(BF16)
        for pair in range(4):
            cols = slice(128 * pair, 128 * pair + 128)
            att, dq, dk, dv = attend_pair(
                projected[:, 128 * pair : 128 * pair + 128],
                projected[:, 512 + 128 * pair : 640 + 128 * pair],
                projected[:, 1024 + 128 * pair : 1152 + 128 * pair],
                grads[:, cols],
                bias[...],
            )
            att_t[cols] = att
            dq_all[:, cols] = dq
            dkv_t[128 * pair : 128 * pair + 128] = dk
            dkv_t[512 + 128 * pair : 640 + 128 * pair] = dv
        normed_t = normed.T
        for r in range(4):
            rows = slice(128 * r, 128 * r + 128)
            grad_q = dot(normed_t[rows], dq_all[...])
            grad_kv = dot_nt(normed_t[rows], dkv_t[...])
            for j in range(12):
                block = grad_q if j < 4 else grad_kv
                at = j if j < 4 else j - 4
                part[pl.ds(1536 * r + j, 128, stride=12), :] = block[:, 128 * at : 128 * at + 128]
            grad_o = dot(att_t[rows], cots)
            for j in range(4):
                part[pl.ds(6144 + 512 * r + j, 128, stride=4), :] = grad_o[
                    :, 128 * j : 128 * j + 128
                ]

        def chunks(at_chip_x, at_chip_y, piece, c):
            blk_of = (at_chip_x % 2) * 4 + at_chip_y
            start = ((blk_of * 16 + 4 * piece) * 4 + (at_chip_x // 2) * 2 + c) * 16
            return jnp.stack(
                [part[pl.ds(pl.multiple_of(start + i * 64, 16), 16), :] for i in range(4)]
            )

        def piece_chunks(piece, first, second, c):
            if piece % 2 == 0:
                return chunks(first, second, piece, c)
            return chunks(second, first, piece, c)

        def along(piece, first):
            if (piece % 2 == 0) == first:
                return x, at_x
            return y, at_y

        zeros, ones, twos, threes = [], [], [], []
        for i in range(4):
            for p in range(4):
                for q in range(4):
                    core_out[i, p, q] = piece_chunks(i, p, q, 1 - core).astype(BF16)
            zeros.append(send(core_out.at[i], core_in.at[i], core_sems, i, mate))
        for i in range(4):
            zeros[i].wait_recv()
            for p in range(4):
                for q in range(4):
                    total = piece_chunks(i, p, q, core) + core_in[i, p, q].astype(F32)
                    out_1[i, p, q] = total.astype(BF16)
            here, at = along(i, True)
            for d in (2, 1, 3):
                to = (here + d) % 4
                ones.append(
                    send(out_1.at[i, to], in_1.at[i, d - 1], one_sems, 3 * i + d - 1, at(to))
                )
            for q in range(4):
                sum_1[i, q] = piece_chunks(i, here, q, core) + core_in[i, here, q].astype(F32)
        for i in range(4):
            for copy in ones[3 * i : 3 * i + 3]:
                copy.wait_recv()
            for q in range(4):
                total = sum_1[i, q]
                for d in range(3):
                    total += in_1[i, d, q].astype(F32)
                sum_1[i, q] = total
                out_2[i, q] = total.astype(BF16)
            here, at = along(i, False)
            for d in (2, 1, 3):
                to = (here + d) % 4
                twos.append(
                    send(out_2.at[i, to], in_2.at[i, d - 1], two_sems, 3 * i + d - 1, at(to))
                )
        for i in range(4):
            for copy in twos[3 * i : 3 * i + 3]:
                copy.wait_recv()
            here, at = along(i, False)
            total = sum_1[i, here]
            for d in range(3):
                total += in_2[i, d].astype(F32)
            z_sum[4 * i : 4 * i + 4] = total
            z_out[4 * i : 4 * i + 4] = total.astype(BF16)
            for k in range(4):
                to = 4 * i + (k + zed) % 4
                copy = remote(
                    z_out.at[to], z_in.at[zed], z_sems.at[0, to], z_sems.at[1, zed], at_z(to)
                )
                other = to != zed
                pl.when(other)(copy.start)
                threes.append((copy, other))

        for copy in weight_copies + passed + zeros + ones + twos:
            copy.wait_send()
        for copy, other in threes:
            pl.when(other)(copy.wait_send)

    total = z_sum[zed]
    for g in range(GROUPS):
        come = place_of(g)
        copy = remote(
            z_in.at[come], z_in.at[come], z_sems.at[0, 0], z_sems.at[1, come], at_z(come)
        )
        pl.when(come != zed)(copy.wait_recv)
    for g in range(GROUPS):
        total += z_in[place_of(g)].astype(F32)
    out[...] = total

    for copy, other in cot_copies + normed_copies:
        pl.when(other)(copy.wait_send)

    @pl.when(blk > 0)
    def _():
        up.wait_send()

    @pl.when(blk < 7)
    def _():
        down.wait_send()


def per_device(features, neighbours, conv_taps, norm_gain, qkv_weight, out_weight, cotangent):
    def pair(count):
        return pltpu.SemaphoreType.DMA((2, count))

    result = pl.pallas_call(
        kernel,
        out_shape=jax.ShapeDtypeStruct(TILE, F32),
        in_specs=[pl.BlockSpec(memory_space=pltpu.HBM)] * 7,
        out_specs=pl.BlockSpec(memory_space=pltpu.VMEM),
        scratch_shapes=[
            pltpu.VMEM((NEAR, 512), BF16),
            pltpu.VMEM((8, BAND), jnp.int32),
            pltpu.VMEM((9, 512), F32),
            pltpu.VMEM((1, 512), F32),
            pltpu.VMEM((GROUPS, GROUP, 512), BF16),
            pltpu.VMEM((16, GROUP, 512), BF16),
            pltpu.VMEM((16, GROUP, 512), BF16),
            pltpu.VMEM((512, 1536), BF16),
            pltpu.VMEM((512, 512), BF16),
            pltpu.VMEM((ROWS, 1536), BF16),
            pltpu.VMEM((ROWS, ROWS), F32),
            pltpu.VMEM((512, ROWS), BF16),
            pltpu.VMEM((ROWS, 512), BF16),
            pltpu.VMEM((1024, ROWS), BF16),
            pltpu.VMEM((8192, 128), F32),
            pltpu.VMEM((4, 4, 4, 4) + TILE, BF16),
            pltpu.VMEM((4, 4, 4, 4) + TILE, BF16),
            pltpu.VMEM((4, 4, 4, 4) + TILE, BF16),
            pltpu.VMEM((4, 3, 4, 4) + TILE, BF16),
            pltpu.VMEM((4, 4, 4) + TILE, F32),
            pltpu.VMEM((4, 4, 4) + TILE, BF16),
            pltpu.VMEM((4, 3, 4) + TILE, BF16),
            pltpu.VMEM((16,) + TILE, F32),
            pltpu.VMEM((16,) + TILE, BF16),
            pltpu.VMEM((16,) + TILE, BF16),
            pltpu.SemaphoreType.DMA((7,)),
            pair(2),
            pair(6),
            pair(16),
            pair(16),
            pair(4),
            pair(12),
            pair(12),
            pair(16),
        ],
        compiler_params=pltpu.CompilerParams(
            collective_id=0, has_side_effects=True, vmem_limit_bytes=60 * 1024 * 1024
        ),
    )(
        features.reshape(BAND, 512),
        neighbours.T,
        conv_taps,
        norm_gain.reshape(1, 512),
        qkv_weight,
        out_weight,
        cotangent.reshape(GROUPS, GROUP, 512),
    )
    return result.reshape(-1)


def solution(mesh):
    return jax.shard_map(
        per_device,
        mesh=mesh,
        in_specs=(
            P("fsdp", "tm", "blk", None),
            P("blk", None),
            P(),
            P(),
            P("fsdp", None),
            P("fsdp", None),
            P("fsdp", "tm", "blk", None),
        ),
        out_specs=P(("blk", "tm", "fsdp")),
        check_vma=False,
    )
```

```python
import jax
import jax.numpy as jnp
from jax import lax
from jax.experimental import pallas as pl
from jax.experimental.pallas import tpu as pltpu
from jax.sharding import PartitionSpec as P

MESH = pl.DeviceIdType.MESH
F32 = jnp.float32
BF16 = jnp.bfloat16
EDGE = 144
BAND = 160
NEAR = 512
GROUP = 16
GROUPS = BAND // GROUP
ROWS = 16 * GROUP
TILE = (16, 128)


def dot(a, b):
    return lax.dot_general(a, b, (((1,), (0,)), ((), ())), preferred_element_type=F32)


def dot_nt(a, b):
    return lax.dot_general(a, b, (((1,), (1,)), ((), ())), preferred_element_type=F32)


def hidden_rows(near, inputs, local, taps):
    rows = inputs.shape[0]
    inputs = inputs.astype(F32)
    spatial = taps[0:1] * inputs
    column = lax.broadcasted_iota(jnp.int32, (rows, NEAR), 1)
    for k in range(8):
        pick = jnp.where(local[:, k : k + 1] == column, 1.0, 0.0).astype(BF16)
        spatial += taps[k + 1 : k + 2] * dot(pick, near)
    return (inputs + spatial).astype(BF16)


def normalized(hidden, gain):
    hidden = hidden.astype(F32)
    inverse = lax.rsqrt(jnp.mean(hidden * hidden, axis=-1, keepdims=True) + 1e-05)
    return (hidden * inverse * gain).astype(BF16)


def causal_bias():
    row = lax.broadcasted_iota(jnp.int32, (ROWS, ROWS), 0)
    col = lax.broadcasted_iota(jnp.int32, (ROWS, ROWS), 1)
    same = row % GROUP == col % GROUP
    return jnp.where(same & (col <= row), 0.0, -1e30).astype(F32)


def attend_pair(q, k, v, g, bias):
    lane = lax.broadcasted_iota(jnp.int32, q.shape, 1)
    sub = lax.broadcasted_iota(jnp.int32, q.shape[::-1], 0)
    q_t, v_t, g_t = q.T, v.T, g.T
    att_t = dq = dk_t = dv_t = 0.0
    for half in range(2):
        ours = lane // 64 == half
        ours_t = sub // 64 == half
        zero = jnp.zeros((), BF16)
        eighth = jnp.asarray(0.125, BF16)
        scores = dot_nt(jnp.where(ours, q * eighth, zero), k) + bias
        raised = jnp.exp(scores - jnp.max(scores, axis=-1, keepdims=True))
        weights = (raised * (1.0 / jnp.sum(raised, axis=-1, keepdims=True))).astype(BF16)
        dprob = dot_nt(jnp.where(ours, g, zero), v)
        wide = weights.astype(F32)
        delta = jnp.sum(wide * dprob, axis=-1, keepdims=True)
        dscore = (wide * (dprob - delta)).astype(BF16)
        att_t += dot_nt(jnp.where(ours_t, v_t, zero), weights)
        dq += dot(dscore, jnp.where(ours, k * eighth, zero))
        dk_t += dot(jnp.where(ours_t, q_t * eighth, zero), dscore)
        dv_t += dot(jnp.where(ours_t, g_t, zero), weights)
    return att_t.astype(BF16), dq.astype(BF16), dk_t.astype(BF16), dv_t.astype(BF16)


def place_of(group):
    lane = group % 5
    return (3 * lane + (group // 5) * (1 + lane // 2 - lane // 4) + 6) % 16


def group_of(zed):
    place = (zed + 10) % 16
    group = jnp.minimum(place // 3, 4) + jnp.where(place % 3 == 0, 0, 5)
    return group, place_of(group) == zed


def kernel(
    features,
    neighbours,
    taps_in,
    gain_in,
    qkv_shard,
    out_shard,
    cotangent,
    out,
    near,
    nearby,
    taps,
    gain,
    normed_out,
    normed_in,
    cot_in,
    qkv_all,
    out_all,
    projected,
    bias,
    att_t,
    dq_all,
    dkv_t,
    part,
    core_out,
    core_in,
    out_1,
    in_1,
    sum_1,
    out_2,
    in_2,
    z_sum,
    z_out,
    z_in,
    local_sems,
    halo_sems,
    weight_sems,
    cot_sems,
    normed_sems,
    core_sems,
    one_sems,
    two_sems,
    z_sems,
):
    blk = lax.axis_index("blk")
    zed = lax.axis_index("tm")
    fsdp = lax.axis_index("fsdp")
    x_lo, y = blk // 4, blk % 4
    x_hi, core = fsdp // 2, fsdp % 2
    x = x_hi * 2 + x_lo
    group, active = group_of(zed)

    def at_x(to):
        return ((to % 2) * 4 + y, zed, (to // 2) * 2 + core)

    def at_y(to):
        return (x_lo * 4 + to, zed, fsdp)

    def at_z(to):
        return (blk, to, fsdp)

    mate = (blk, zed, x_hi * 2 + 1 - core)
    facing = ((1 - x_lo) * 4 + y, zed, (1 - x_hi) * 2 + core)
    partners = [mate]
    partners += [at_x((x + d) % 4) for d in (1, 2, 3)]
    partners += [at_y((y + d) % 4) for d in (1, 2, 3)]
    partners += [at_z((zed + d) % 16) for d in range(1, 16)]
    barrier = pltpu.get_barrier_semaphore()

    def greet(to):
        pl.semaphore_signal(barrier, inc=1, device_id=to, device_id_type=MESH)

    for partner in partners:
        greet(partner)

    @pl.when(blk == 3)
    def _():
        greet((4, zed, fsdp))

    @pl.when(blk == 4)
    def _():
        greet((3, zed, fsdp))

    def remote(src, dst, send_sem, recv_sem, to):
        return pltpu.make_async_remote_copy(
            src_ref=src,
            dst_ref=dst,
            send_sem=send_sem,
            recv_sem=recv_sem,
            device_id=to,
            device_id_type=MESH,
        )

    def send(src, dst, sems, slot, to):
        copy = remote(src, dst, sems.at[0, slot], sems.at[1, slot], to)
        copy.start()
        return copy

    shard = pl.ds(pl.multiple_of(fsdp * 128, 128), 128)
    owned = [
        pltpu.make_async_copy(src, dst, local_sems.at[i])
        for i, (src, dst) in enumerate(
            (
                (features, near.at[EDGE : EDGE + BAND]),
                (neighbours, nearby),
                (taps_in, taps),
                (gain_in, gain),
            )
        )
    ]
    held = [
        pltpu.make_async_copy(src, dst, local_sems.at[4 + i])
        for i, (src, dst) in enumerate(
            (
                (cotangent.at[group], cot_in.at[zed]),
                (qkv_shard, qkv_all.at[shard]),
                (out_shard, out_all.at[shard]),
            )
        )
    ]
    for copy in owned:
        copy.start()

    @pl.when(active)
    def _():
        for copy in held:
            copy.start()

    near[2 * EDGE + BAND :] = jnp.zeros((NEAR - 2 * EDGE - BAND, 512), BF16)
    z_in[...] = jnp.zeros_like(z_in)

    @pl.when(blk == 0)
    def _():
        near[0:EDGE] = jnp.zeros((EDGE, 512), BF16)

    @pl.when(blk == 7)
    def _():
        near[EDGE + BAND : 2 * EDGE + BAND] = jnp.zeros((EDGE, 512), BF16)

    @pl.when(active)
    def _():
        bias[...] = causal_bias()

    @pl.when(jnp.logical_not(active))
    def _():
        z_sum[...] = jnp.zeros_like(z_sum)

    for copy in owned:
        copy.wait()

    extra = jnp.where((blk == 3) | (blk == 4), 1, 0)
    pl.semaphore_wait(barrier, len(partners) + extra)

    up = remote(
        near.at[EDGE : 2 * EDGE],
        near.at[EDGE + BAND : 2 * EDGE + BAND],
        halo_sems.at[0, 0],
        halo_sems.at[1, 0],
        (jnp.maximum(blk - 1, 0), zed, fsdp),
    )
    down = remote(
        near.at[BAND : EDGE + BAND],
        near.at[0:EDGE],
        halo_sems.at[0, 1],
        halo_sems.at[1, 1],
        (jnp.minimum(blk + 1, 7), zed, fsdp),
    )

    @pl.when(blk > 0)
    def _():
        up.start()

    @pl.when(blk < 7)
    def _():
        down.start()

    def exchange(source, target, sems, first):
        copies = []
        farthest = ((zed + 18) % 16) // 3
        for k in (0, 1, 4, 2, 3):
            theirs = first + (farthest + k) % 5
            to = place_of(theirs)
            copy = remote(
                source.at[theirs], target.at[zed], sems.at[0, theirs], sems.at[1, zed], at_z(to)
            )
            other = to != zed
            copies.append((copy, other))
            pl.when(other)(copy.start)
        return copies

    def arrivals(target, sems):
        for come in range(16):
            copy = remote(
                target.at[come], target.at[come], sems.at[0, 0], sems.at[1, come], at_z(come)
            )
            pl.when(come != zed)(copy.wait_recv)

    weight_copies = [
        remote(src, dst.at[shard], weight_sems.at[0, i], weight_sems.at[1, i], to)
        for i, (src, dst, to) in enumerate(
            (
                (qkv_shard, qkv_all, facing),
                (out_shard, out_all, facing),
                (qkv_shard, qkv_all, mate),
                (out_shard, out_all, mate),
            )
        )
    ]

    @pl.when(active)
    def _():
        for copy in weight_copies:
            copy.start()

    cot_copies = [
        pair
        for first in (0, 5)
        for pair in exchange(cotangent, cot_in, cot_sems, first)
    ]
    local_all = nearby[...].T - (blk * BAND - EDGE)

    @pl.when(blk > 0)
    def _():
        down.wait_recv()

    @pl.when(blk < 7)
    def _():
        up.wait_recv()

    normed_copies = []
    half_rows, half_groups = BAND // 2, GROUPS // 2
    for half in range(2):
        rows = slice(half * half_rows, (half + 1) * half_rows)
        own = near[EDGE + half * half_rows : EDGE + (half + 1) * half_rows]
        hidden = hidden_rows(near[...], own, local_all[rows], taps)
        normed_out[half * half_groups : (half + 1) * half_groups] = normalized(
            hidden, gain[...]
        ).reshape(half_groups, GROUP, 512)
        normed_copies += exchange(
            normed_out, normed_in, normed_sems, half * half_groups
        )

    @pl.when(active)
    def _():
        normed_in[zed] = normed_out[group]
        facing_shard = pl.ds(pl.multiple_of(((1 - x_hi) * 2 + core) * 128, 128), 128)
        weight_copies[0].wait_recv()
        weight_copies[1].wait_recv()
        passed = [
            send(qkv_all.at[facing_shard], qkv_all.at[facing_shard], weight_sems, 4, mate),
            send(out_all.at[facing_shard], out_all.at[facing_shard], weight_sems, 5, mate),
        ]
        for copy in held:
            copy.wait()
        for copy in weight_copies[2:] + passed:
            copy.wait_recv()
        arrivals(cot_in, cot_sems)
        cots = cot_in[...].reshape(ROWS, 512)
        grads = dot_nt(cots, out_all[...]).astype(BF16)
        arrivals(normed_in, normed_sems)
        normed = normed_in[...].reshape(ROWS, 512)
        for j in range(6):
            block = slice(256 * j, 256 * j + 256)
            projected[:, block] = dot(normed, qkv_all[:, block]).astype(BF16)
        for pair in range(4):
            cols = slice(128 * pair, 128 * pair + 128)
            att, dq, dk, dv = attend_pair(
                projected[:, 128 * pair : 128 * pair + 128],
                projected[:, 512 + 128 * pair : 640 + 128 * pair],
                projected[:, 1024 + 128 * pair : 1152 + 128 * pair],
                grads[:, cols],
                bias[...],
            )
            att_t[cols] = att
            dq_all[:, cols] = dq
            dkv_t[128 * pair : 128 * pair + 128] = dk
            dkv_t[512 + 128 * pair : 640 + 128 * pair] = dv
        normed_t = normed.T
        for r in range(4):
            rows = slice(128 * r, 128 * r + 128)
            grad_q = dot(normed_t[rows], dq_all[...])
            grad_kv = dot_nt(normed_t[rows], dkv_t[...])
            for j in range(12):
                block = grad_q if j < 4 else grad_kv
                at = j if j < 4 else j - 4
                part[pl.ds(1536 * r + j, 128, stride=12), :] = block[:, 128 * at : 128 * at + 128]
            grad_o = dot(att_t[rows], cots)
            for j in range(4):
                part[pl.ds(6144 + 512 * r + j, 128, stride=4), :] = grad_o[
                    :, 128 * j : 128 * j + 128
                ]

        def chunks(at_chip_x, at_chip_y, piece, c):
            blk_of = (at_chip_x % 2) * 4 + at_chip_y
            start = ((blk_of * 16 + 4 * piece) * 4 + (at_chip_x // 2) * 2 + c) * 16
            return jnp.stack(
                [part[pl.ds(pl.multiple_of(start + i * 64, 16), 16), :] for i in range(4)]
            )

        def piece_chunks(piece, first, second, c):
            if piece % 2 == 0:
                return chunks(first, second, piece, c)
            return chunks(second, first, piece, c)

        def along(piece, first):
            if (piece % 2 == 0) == first:
                return x, at_x
            return y, at_y

        zeros, ones, twos, threes = [], [], [], []
        for i in range(4):
            for p in range(4):
                for q in range(4):
                    core_out[i, p, q] = piece_chunks(i, p, q, 1 - core).astype(BF16)
            zeros.append(send(core_out.at[i], core_in.at[i], core_sems, i, mate))
        for i in range(4):
            zeros[i].wait_recv()
            for p in range(4):
                for q in range(4):
                    total = piece_chunks(i, p, q, core) + core_in[i, p, q].astype(F32)
                    out_1[i, p, q] = total.astype(BF16)
            here, at = along(i, True)
            for d in (2, 1, 3):
                to = (here + d) % 4
                ones.append(
                    send(out_1.at[i, to], in_1.at[i, d - 1], one_sems, 3 * i + d - 1, at(to))
                )
            for q in range(4):
                sum_1[i, q] = piece_chunks(i, here, q, core) + core_in[i, here, q].astype(F32)
        for i in range(4):
            for copy in ones[3 * i : 3 * i + 3]:
                copy.wait_recv()
            for q in range(4):
                total = sum_1[i, q]
                for d in range(3):
                    total += in_1[i, d, q].astype(F32)
                sum_1[i, q] = total
                out_2[i, q] = total.astype(BF16)
            here, at = along(i, False)
            for d in (2, 1, 3):
                to = (here + d) % 4
                twos.append(
                    send(out_2.at[i, to], in_2.at[i, d - 1], two_sems, 3 * i + d - 1, at(to))
                )
        for i in range(4):
            for copy in twos[3 * i : 3 * i + 3]:
                copy.wait_recv()
            here, at = along(i, False)
            total = sum_1[i, here]
            for d in range(3):
                total += in_2[i, d].astype(F32)
            z_sum[4 * i : 4 * i + 4] = total
            z_out[4 * i : 4 * i + 4] = total.astype(BF16)
            for k in range(4):
                to = 4 * i + (k + zed) % 4
                copy = remote(
                    z_out.at[to], z_in.at[zed], z_sems.at[0, to], z_sems.at[1, zed], at_z(to)
                )
                other = to != zed
                pl.when(other)(copy.start)
                threes.append((copy, other))

        for copy in weight_copies + passed + zeros + ones + twos:
            copy.wait_send()
        for copy, other in threes:
            pl.when(other)(copy.wait_send)

    for copy, other in cot_copies + normed_copies:
        pl.when(other)(copy.wait_send)

    @pl.when(blk > 0)
    def _():
        up.wait_send()

    @pl.when(blk < 7)
    def _():
        down.wait_send()

    total = z_sum[zed]
    for g in range(GROUPS):
        come = place_of(g)
        copy = remote(
            z_in.at[come], z_in.at[come], z_sems.at[0, 0], z_sems.at[1, come], at_z(come)
        )
        pl.when(come != zed)(copy.wait_recv)
    for g in range(GROUPS):
        total += z_in[place_of(g)].astype(F32)
    out[...] = total


def per_device(features, neighbours, conv_taps, norm_gain, qkv_weight, out_weight, cotangent):
    def pair(count):
        return pltpu.SemaphoreType.DMA((2, count))

    result = pl.pallas_call(
        kernel,
        out_shape=jax.ShapeDtypeStruct(TILE, F32),
        in_specs=[pl.BlockSpec(memory_space=pltpu.HBM)] * 7,
        out_specs=pl.BlockSpec(memory_space=pltpu.VMEM),
        scratch_shapes=[
            pltpu.VMEM((NEAR, 512), BF16),
            pltpu.VMEM((8, BAND), jnp.int32),
            pltpu.VMEM((9, 512), F32),
            pltpu.VMEM((1, 512), F32),
            pltpu.VMEM((GROUPS, GROUP, 512), BF16),
            pltpu.VMEM((16, GROUP, 512), BF16),
            pltpu.VMEM((16, GROUP, 512), BF16),
            pltpu.VMEM((512, 1536), BF16),
            pltpu.VMEM((512, 512), BF16),
            pltpu.VMEM((ROWS, 1536), BF16),
            pltpu.VMEM((ROWS, ROWS), F32),
            pltpu.VMEM((512, ROWS), BF16),
            pltpu.VMEM((ROWS, 512), BF16),
            pltpu.VMEM((1024, ROWS), BF16),
            pltpu.VMEM((8192, 128), F32),
            pltpu.VMEM((4, 4, 4, 4) + TILE, BF16),
            pltpu.VMEM((4, 4, 4, 4) + TILE, BF16),
            pltpu.VMEM((4, 4, 4, 4) + TILE, BF16),
            pltpu.VMEM((4, 3, 4, 4) + TILE, BF16),
            pltpu.VMEM((4, 4, 4) + TILE, F32),
            pltpu.VMEM((4, 4, 4) + TILE, BF16),
            pltpu.VMEM((4, 3, 4) + TILE, BF16),
            pltpu.VMEM((16,) + TILE, F32),
            pltpu.VMEM((16,) + TILE, BF16),
            pltpu.VMEM((16,) + TILE, BF16),
            pltpu.SemaphoreType.DMA((7,)),
            pair(2),
            pair(6),
            pair(16),
            pair(16),
            pair(4),
            pair(12),
            pair(12),
            pair(16),
        ],
        compiler_params=pltpu.CompilerParams(
            collective_id=0, has_side_effects=True, vmem_limit_bytes=60 * 1024 * 1024
        ),
    )(
        features.reshape(BAND, 512),
        neighbours.T,
        conv_taps,
        norm_gain.reshape(1, 512),
        qkv_weight,
        out_weight,
        cotangent.reshape(GROUPS, GROUP, 512),
    )
    return result.reshape(-1)


def solution(mesh):
    return jax.shard_map(
        per_device,
        mesh=mesh,
        in_specs=(
            P("fsdp", "tm", "blk", None),
            P("blk", None),
            P(),
            P(),
            P("fsdp", None),
            P("fsdp", None),
            P("fsdp", "tm", "blk", None),
        ),
        out_specs=P(("blk", "tm", "fsdp")),
        check_vma=False,
    )
```

```python
import jax
import jax.numpy as jnp
from jax import lax
from jax.experimental import pallas as pl
from jax.experimental.pallas import tpu as pltpu
from jax.sharding import PartitionSpec as P

MESH = pl.DeviceIdType.MESH
F32 = jnp.float32
BF16 = jnp.bfloat16
EDGE = 144
BAND = 160
NEAR = 512
GROUP = 16
GROUPS = BAND // GROUP
ROWS = 16 * GROUP
TILE = (16, 128)


def dot(a, b):
    return lax.dot_general(a, b, (((1,), (0,)), ((), ())), preferred_element_type=F32)


def dot_nt(a, b):
    return lax.dot_general(a, b, (((1,), (1,)), ((), ())), preferred_element_type=F32)


def hidden_rows(near, inputs, local, taps):
    rows = inputs.shape[0]
    inputs = inputs.astype(F32)
    spatial = taps[0:1] * inputs
    column = lax.broadcasted_iota(jnp.int32, (rows, NEAR), 1)
    for k in range(8):
        pick = jnp.where(local[:, k : k + 1] == column, 1.0, 0.0).astype(BF16)
        spatial += taps[k + 1 : k + 2] * dot(pick, near)
    return (inputs + spatial).astype(BF16)


def normalized(hidden, gain):
    hidden = hidden.astype(F32)
    inverse = lax.rsqrt(jnp.mean(hidden * hidden, axis=-1, keepdims=True) + 1e-05)
    return (hidden * inverse * gain).astype(BF16)


def causal_bias():
    row = lax.broadcasted_iota(jnp.int32, (ROWS, ROWS), 0)
    col = lax.broadcasted_iota(jnp.int32, (ROWS, ROWS), 1)
    same = row % GROUP == col % GROUP
    return jnp.where(same & (col <= row), 0.0, -1e30).astype(F32)


def attend_pair(q, k, v, g, bias):
    lane = lax.broadcasted_iota(jnp.int32, q.shape, 1)
    sub = lax.broadcasted_iota(jnp.int32, q.shape[::-1], 0)
    q_t, v_t, g_t = q.T, v.T, g.T
    att_t = dq = dk_t = dv_t = 0.0
    for half in range(2):
        ours = lane // 64 == half
        ours_t = sub // 64 == half
        zero = jnp.zeros((), BF16)
        eighth = jnp.asarray(0.125, BF16)
        scores = dot_nt(jnp.where(ours, q * eighth, zero), k) + bias
        raised = jnp.exp(scores - jnp.max(scores, axis=-1, keepdims=True))
        weights = (raised * (1.0 / jnp.sum(raised, axis=-1, keepdims=True))).astype(BF16)
        dprob = dot_nt(jnp.where(ours, g, zero), v)
        wide = weights.astype(F32)
        delta = jnp.sum(wide * dprob, axis=-1, keepdims=True)
        dscore = (wide * (dprob - delta)).astype(BF16)
        att_t += dot_nt(jnp.where(ours_t, v_t, zero), weights)
        dq += dot(dscore, jnp.where(ours, k * eighth, zero))
        dk_t += dot(jnp.where(ours_t, q_t * eighth, zero), dscore)
        dv_t += dot(jnp.where(ours_t, g_t, zero), weights)
    return att_t.astype(BF16), dq.astype(BF16), dk_t.astype(BF16), dv_t.astype(BF16)


def place_of(group):
    lane = group % 5
    return (3 * lane + (group // 5) * (1 + lane // 2 - lane // 4) + 6) % 16


def group_of(zed):
    place = (zed + 10) % 16
    group = jnp.minimum(place // 3, 4) + jnp.where(place % 3 == 0, 0, 5)
    return group, place_of(group) == zed


def kernel(
    features,
    neighbours,
    taps_in,
    gain_in,
    qkv_shard,
    out_shard,
    cotangent,
    out,
    near,
    nearby,
    taps,
    gain,
    normed_out,
    normed_in,
    cot_in,
    qkv_all,
    out_all,
    projected,
    bias,
    att_t,
    dq_all,
    dkv_t,
    part,
    core_out,
    core_in,
    out_1,
    in_1,
    sum_1,
    out_2,
    in_2,
    z_sum,
    z_out,
    z_in,
    local_sems,
    halo_sems,
    weight_sems,
    cot_sems,
    normed_sems,
    core_sems,
    one_sems,
    two_sems,
    z_sems,
):
    blk = lax.axis_index("blk")
    zed = lax.axis_index("tm")
    fsdp = lax.axis_index("fsdp")
    x_lo, y = blk // 4, blk % 4
    x_hi, core = fsdp // 2, fsdp % 2
    x = x_hi * 2 + x_lo
    group, active = group_of(zed)

    def at_x(to):
        return ((to % 2) * 4 + y, zed, (to // 2) * 2 + core)

    def at_y(to):
        return (x_lo * 4 + to, zed, fsdp)

    def at_z(to):
        return (blk, to, fsdp)

    mate = (blk, zed, x_hi * 2 + 1 - core)
    facing = ((1 - x_lo) * 4 + y, zed, (1 - x_hi) * 2 + core)
    partners = [mate]
    partners += [at_x((x + d) % 4) for d in (1, 2, 3)]
    partners += [at_y((y + d) % 4) for d in (1, 2, 3)]
    partners += [at_z((zed + d) % 16) for d in range(1, 16)]
    barrier = pltpu.get_barrier_semaphore()

    def greet(to):
        pl.semaphore_signal(barrier, inc=1, device_id=to, device_id_type=MESH)

    for partner in partners:
        greet(partner)

    @pl.when(blk == 3)
    def _():
        greet((4, zed, fsdp))

    @pl.when(blk == 4)
    def _():
        greet((3, zed, fsdp))

    def remote(src, dst, send_sem, recv_sem, to):
        return pltpu.make_async_remote_copy(
            src_ref=src,
            dst_ref=dst,
            send_sem=send_sem,
            recv_sem=recv_sem,
            device_id=to,
            device_id_type=MESH,
        )

    def send(src, dst, sems, slot, to):
        copy = remote(src, dst, sems.at[0, slot], sems.at[1, slot], to)
        copy.start()
        return copy

    shard = pl.ds(pl.multiple_of(fsdp * 128, 128), 128)
    owned = [
        pltpu.make_async_copy(src, dst, local_sems.at[i])
        for i, (src, dst) in enumerate(
            (
                (features, near.at[EDGE : EDGE + BAND]),
                (neighbours, nearby),
                (taps_in, taps),
                (gain_in, gain),
            )
        )
    ]
    held = [
        pltpu.make_async_copy(src, dst, local_sems.at[4 + i])
        for i, (src, dst) in enumerate(
            (
                (cotangent.at[group], cot_in.at[zed]),
                (qkv_shard, qkv_all.at[shard]),
                (out_shard, out_all.at[shard]),
            )
        )
    ]
    for copy in owned:
        copy.start()

    @pl.when(active)
    def _():
        for copy in held:
            copy.start()

    extra = jnp.where((blk == 3) | (blk == 4), 1, 0)
    pl.semaphore_wait(barrier, len(partners) + extra)

    up = remote(
        features.at[0:EDGE],
        near.at[EDGE + BAND : 2 * EDGE + BAND],
        halo_sems.at[0, 0],
        halo_sems.at[1, 0],
        (jnp.maximum(blk - 1, 0), zed, fsdp),
    )
    down = remote(
        features.at[BAND - EDGE : BAND],
        near.at[0:EDGE],
        halo_sems.at[0, 1],
        halo_sems.at[1, 1],
        (jnp.minimum(blk + 1, 7), zed, fsdp),
    )

    @pl.when(blk > 0)
    def _():
        up.start()

    @pl.when(blk < 7)
    def _():
        down.start()

    def exchange(source, target, sems, first):
        copies = []
        farthest = ((zed + 18) % 16) // 3
        for k in (0, 1, 4, 2, 3):
            theirs = first + (farthest + k) % 5
            to = place_of(theirs)
            copy = remote(
                source.at[theirs], target.at[zed], sems.at[0, theirs], sems.at[1, zed], at_z(to)
            )
            other = to != zed
            copies.append((copy, other))
            pl.when(other)(copy.start)
        return copies

    def arrivals(target, sems):
        for come in range(16):
            copy = remote(
                target.at[come], target.at[come], sems.at[0, 0], sems.at[1, come], at_z(come)
            )
            pl.when(come != zed)(copy.wait_recv)

    weight_copies = [
        remote(src, dst.at[shard], weight_sems.at[0, i], weight_sems.at[1, i], to)
        for i, (src, dst, to) in enumerate(
            (
                (qkv_shard, qkv_all, facing),
                (out_shard, out_all, facing),
                (qkv_shard, qkv_all, mate),
                (out_shard, out_all, mate),
            )
        )
    ]

    @pl.when(active)
    def _():
        for copy in weight_copies:
            copy.start()

    cot_copies = [
        pair
        for first in (0, 5)
        for pair in exchange(cotangent, cot_in, cot_sems, first)
    ]
    near[2 * EDGE + BAND :] = jnp.zeros((NEAR - 2 * EDGE - BAND, 512), BF16)
    z_in[zed] = jnp.zeros(TILE, BF16)

    @pl.when(blk == 0)
    def _():
        near[0:EDGE] = jnp.zeros((EDGE, 512), BF16)

    @pl.when(blk == 7)
    def _():
        near[EDGE + BAND : 2 * EDGE + BAND] = jnp.zeros((EDGE, 512), BF16)

    @pl.when(active)
    def _():
        bias[...] = causal_bias()

    @pl.when(jnp.logical_not(active))
    def _():
        z_sum[...] = jnp.zeros_like(z_sum)

    for copy in owned:
        copy.wait()
    local_all = nearby[...].T - (blk * BAND - EDGE)

    @pl.when(blk > 0)
    def _():
        down.wait_recv()

    @pl.when(blk < 7)
    def _():
        up.wait_recv()

    normed_copies = []
    half_rows, half_groups = BAND // 2, GROUPS // 2
    for half in range(2):
        rows = slice(half * half_rows, (half + 1) * half_rows)
        own = near[EDGE + half * half_rows : EDGE + (half + 1) * half_rows]
        hidden = hidden_rows(near[...], own, local_all[rows], taps)
        normed_out[half * half_groups : (half + 1) * half_groups] = normalized(
            hidden, gain[...]
        ).reshape(half_groups, GROUP, 512)
        normed_copies += exchange(
            normed_out, normed_in, normed_sems, half * half_groups
        )

    @pl.when(active)
    def _():
        normed_in[zed] = normed_out[group]
        facing_shard = pl.ds(pl.multiple_of(((1 - x_hi) * 2 + core) * 128, 128), 128)
        weight_copies[0].wait_recv()
        weight_copies[1].wait_recv()
        passed = [
            send(qkv_all.at[facing_shard], qkv_all.at[facing_shard], weight_sems, 4, mate),
            send(out_all.at[facing_shard], out_all.at[facing_shard], weight_sems, 5, mate),
        ]
        for copy in held:
            copy.wait()
        for copy in weight_copies[2:] + passed:
            copy.wait_recv()
        arrivals(cot_in, cot_sems)
        cots = cot_in[...].reshape(ROWS, 512)
        grads = dot_nt(cots, out_all[...]).astype(BF16)
        arrivals(normed_in, normed_sems)
        normed = normed_in[...].reshape(ROWS, 512)
        for j in range(6):
            block = slice(256 * j, 256 * j + 256)
            projected[:, block] = dot(normed, qkv_all[:, block]).astype(BF16)
        for pair in range(4):
            cols = slice(128 * pair, 128 * pair + 128)
            att, dq, dk, dv = attend_pair(
                projected[:, 128 * pair : 128 * pair + 128],
                projected[:, 512 + 128 * pair : 640 + 128 * pair],
                projected[:, 1024 + 128 * pair : 1152 + 128 * pair],
                grads[:, cols],
                bias[...],
            )
            att_t[cols] = att
            dq_all[:, cols] = dq
            dkv_t[128 * pair : 128 * pair + 128] = dk
            dkv_t[512 + 128 * pair : 640 + 128 * pair] = dv
        normed_t = normed.T
        for r in range(4):
            rows = slice(128 * r, 128 * r + 128)
            grad_q = dot(normed_t[rows], dq_all[...])
            grad_kv = dot_nt(normed_t[rows], dkv_t[...])
            for j in range(12):
                block = grad_q if j < 4 else grad_kv
                at = j if j < 4 else j - 4
                part[pl.ds(1536 * r + j, 128, stride=12), :] = block[:, 128 * at : 128 * at + 128]
            grad_o = dot(att_t[rows], cots)
            for j in range(4):
                part[pl.ds(6144 + 512 * r + j, 128, stride=4), :] = grad_o[
                    :, 128 * j : 128 * j + 128
                ]

        def chunks(at_chip_x, at_chip_y, piece, c):
            blk_of = (at_chip_x % 2) * 4 + at_chip_y
            start = ((blk_of * 16 + 4 * piece) * 4 + (at_chip_x // 2) * 2 + c) * 16
            return jnp.stack(
                [part[pl.ds(pl.multiple_of(start + i * 64, 16), 16), :] for i in range(4)]
            )

        def piece_chunks(piece, first, second, c):
            if piece % 2 == 0:
                return chunks(first, second, piece, c)
            return chunks(second, first, piece, c)

        def along(piece, first):
            if (piece % 2 == 0) == first:
                return x, at_x
            return y, at_y

        zeros, ones, twos, threes = [], [], [], []
        for i in range(4):
            for p in range(4):
                for q in range(4):
                    core_out[i, p, q] = piece_chunks(i, p, q, 1 - core).astype(BF16)
            zeros.append(send(core_out.at[i], core_in.at[i], core_sems, i, mate))
        for i in range(4):
            zeros[i].wait_recv()
            for p in range(4):
                for q in range(4):
                    total = piece_chunks(i, p, q, core) + core_in[i, p, q].astype(F32)
                    out_1[i, p, q] = total.astype(BF16)
            here, at = along(i, True)
            for d in (2, 1, 3):
                to = (here + d) % 4
                ones.append(
                    send(out_1.at[i, to], in_1.at[i, d - 1], one_sems, 3 * i + d - 1, at(to))
                )
            for q in range(4):
                sum_1[i, q] = piece_chunks(i, here, q, core) + core_in[i, here, q].astype(F32)
        def send_second(i):
            for copy in ones[3 * i : 3 * i + 3]:
                copy.wait_recv()
            for q in range(4):
                total = sum_1[i, q]
                for d in range(3):
                    total += in_1[i, d, q].astype(F32)
                sum_1[i, q] = total
                out_2[i, q] = total.astype(BF16)
            here, at = along(i, False)
            for d in (2, 1, 3):
                to = (here + d) % 4
                twos.append(
                    send(out_2.at[i, to], in_2.at[i, d - 1], two_sems, 3 * i + d - 1, at(to))
                )

        def send_third(i):
            for copy in twos[3 * i : 3 * i + 3]:
                copy.wait_recv()
            here, at = along(i, False)
            total = sum_1[i, here]
            for d in range(3):
                total += in_2[i, d].astype(F32)
            z_sum[4 * i : 4 * i + 4] = total
            z_out[4 * i : 4 * i + 4] = total.astype(BF16)
            for k in range(4):
                to = 4 * i + (k + zed) % 4
                copy = remote(
                    z_out.at[to], z_in.at[zed], z_sems.at[0, to], z_sems.at[1, zed], at_z(to)
                )
                other = to != zed
                pl.when(other)(copy.start)
                threes.append((copy, other))

        send_second(0)
        send_second(1)
        send_third(0)
        send_second(2)
        send_third(1)
        send_second(3)
        send_third(2)
        send_third(3)

        for copy in weight_copies + passed + zeros + ones + twos:
            copy.wait_send()
        for copy, other in threes:
            pl.when(other)(copy.wait_send)

    for copy, other in cot_copies + normed_copies:
        pl.when(other)(copy.wait_send)

    @pl.when(blk > 0)
    def _():
        up.wait_send()

    @pl.when(blk < 7)
    def _():
        down.wait_send()

    total = z_sum[zed]
    for g in range(GROUPS):
        come = place_of(g)
        copy = remote(
            z_in.at[come], z_in.at[come], z_sems.at[0, 0], z_sems.at[1, come], at_z(come)
        )
        pl.when(come != zed)(copy.wait_recv)
    for g in range(GROUPS):
        total += z_in[place_of(g)].astype(F32)
    out[...] = total


def per_device(features, neighbours, conv_taps, norm_gain, qkv_weight, out_weight, cotangent):
    def pair(count):
        return pltpu.SemaphoreType.DMA((2, count))

    result = pl.pallas_call(
        kernel,
        out_shape=jax.ShapeDtypeStruct(TILE, F32),
        in_specs=[pl.BlockSpec(memory_space=pltpu.HBM)] * 7,
        out_specs=pl.BlockSpec(memory_space=pltpu.VMEM),
        scratch_shapes=[
            pltpu.VMEM((NEAR, 512), BF16),
            pltpu.VMEM((8, BAND), jnp.int32),
            pltpu.VMEM((9, 512), F32),
            pltpu.VMEM((1, 512), F32),
            pltpu.VMEM((GROUPS, GROUP, 512), BF16),
            pltpu.VMEM((16, GROUP, 512), BF16),
            pltpu.VMEM((16, GROUP, 512), BF16),
            pltpu.VMEM((512, 1536), BF16),
            pltpu.VMEM((512, 512), BF16),
            pltpu.VMEM((ROWS, 1536), BF16),
            pltpu.VMEM((ROWS, ROWS), F32),
            pltpu.VMEM((512, ROWS), BF16),
            pltpu.VMEM((ROWS, 512), BF16),
            pltpu.VMEM((1024, ROWS), BF16),
            pltpu.VMEM((8192, 128), F32),
            pltpu.VMEM((4, 4, 4, 4) + TILE, BF16),
            pltpu.VMEM((4, 4, 4, 4) + TILE, BF16),
            pltpu.VMEM((4, 4, 4, 4) + TILE, BF16),
            pltpu.VMEM((4, 3, 4, 4) + TILE, BF16),
            pltpu.VMEM((4, 4, 4) + TILE, F32),
            pltpu.VMEM((4, 4, 4) + TILE, BF16),
            pltpu.VMEM((4, 3, 4) + TILE, BF16),
            pltpu.VMEM((16,) + TILE, F32),
            pltpu.VMEM((16,) + TILE, BF16),
            pltpu.VMEM((16,) + TILE, BF16),
            pltpu.SemaphoreType.DMA((7,)),
            pair(2),
            pair(6),
            pair(16),
            pair(16),
            pair(4),
            pair(12),
            pair(12),
            pair(16),
        ],
        compiler_params=pltpu.CompilerParams(
            collective_id=0, has_side_effects=True, vmem_limit_bytes=60 * 1024 * 1024
        ),
    )(
        features.reshape(BAND, 512),
        neighbours.T,
        conv_taps,
        norm_gain.reshape(1, 512),
        qkv_weight,
        out_weight,
        cotangent.reshape(GROUPS, GROUP, 512),
    )
    return result.reshape(-1)


def solution(mesh):
    return jax.shard_map(
        per_device,
        mesh=mesh,
        in_specs=(
            P("fsdp", "tm", "blk", None),
            P("blk", None),
            P(),
            P(),
            P("fsdp", None),
            P("fsdp", None),
            P("fsdp", "tm", "blk", None),
        ),
        out_specs=P(("blk", "tm", "fsdp")),
        check_vma=False,
    )
```
